32 devices in a mesh: row: 8 (over z, core), col: 4 (over y, x).
Axes of the slice: x: 2, y: 2, z: 4, core: 2. Of those that a mesh axis runs over, the one named last changes fastest.
Arguments:
- a_blocks: bfloat16 [8, 4, 32, 128, 128], P('row', 'col'), may hold values from -6 to 6
- a_coord: int32 [8, 4, 32, 2], P('row', 'col'), may hold values from -1 to 31, as said below
- b_blocks: bfloat16 [8, 4, 32, 128, 128], P('row', 'col'), may hold values from -0.125 to 0.125
- b_coord: int32 [8, 4, 32, 2], P('row', 'col'), may hold values from -1 to 31, as said below
- c_mask: int32 [32, 32], P('row', 'col'), may hold values 0 or 1
Outputs:
- c_blocks: float32 [4096, 4096], P('row', 'col')
The draws below stay inside these ranges and needn't reach their ends.
Inputs may be any that keep to these rules, and one draw needn't show every extreme that they name: `a_coord`: entry [i, s, t] holds the block row and block column of the block in slot t of device (i, s), or -1 in both for an empty slot. Its block row lies in i * 4 to (i + 1) * 4 - 1. With p = column // 4, slot t lies in t // 8 = (p - i) mod 4. No block is named twice. `b_coord`: entry [s, j, t] holds the block row and block column of the block in slot t of device (s, j), or -1 in both for an empty slot. Its block column lies in j * 8 to (j + 1) * 8 - 1. With p = row // 4, slot t lies in t // 4 = (p - j) mod 8. No block is named twice.
All inputs are finite; a program needn't handle non-finite values. No bound on the sum of `c_mask` on one device may be relied on, other than what follows from the above.
Results may differ from the reference program's by a relative error of at most 0.0003.
Values may be sent and summed in bfloat16 or wider, within the bound.
A program may use at most 64 MiB of HBM per device.

```python
import jax
import jax.numpy as jnp

BS = 128
MB = 4
NB = 32
NC = 8
NPOS = 32
CAPA = 8
CAPB = 4
SLOTS_A = 32
SLOTS_B = 32
N_ROW = 8
N_COL = 4


def draw_a_coord(key, part):
    key_perm, key_rate, key_full, key_roll = jax.random.split(key, 4)
    total_slots = N_COL * CAPA
    perm_keys = jax.random.split(key_perm, N_ROW * N_COL)
    orders = jax.vmap(lambda single: jax.random.permutation(single, total_slots))(perm_keys)
    orders = orders.reshape(N_ROW, N_COL, N_COL, CAPA)
    rates = jax.random.randint(key_rate, (N_ROW, N_COL, 1, 1), 35, 101)
    chosen = jax.random.randint(key_full, (N_ROW, 1, 1, 1), 0, N_COL)
    rolls = jax.random.randint(key_roll, (N_ROW, N_COL, N_COL, CAPA), 0, 100)
    target = jnp.arange(N_COL).reshape(1, N_COL, 1, 1)
    grid_rows = jnp.arange(N_ROW).reshape(N_ROW, 1, 1, 1)
    is_live = (orders < NPOS) & ((rolls < rates) | (target == chosen))
    member = orders // (MB * MB)
    local_row = orders // MB % MB
    local_col = orders % MB
    panel_index = (grid_rows + target) % N_COL + N_COL * member
    block_row = jnp.where(is_live, grid_rows * MB + local_row, -1)
    block_col = jnp.where(is_live, panel_index * MB + local_col, -1)
    stacked = jnp.stack([block_row, block_col], axis=-1)
    return stacked.transpose(0, 2, 1, 3, 4).reshape(N_ROW, N_COL, N_COL * CAPA, 2).astype(jnp.int32)


def draw_b_coord(key, part):
    key_perm, key_rate, key_full, key_roll = jax.random.split(key, 4)
    total_slots = N_ROW * CAPB
    perm_keys = jax.random.split(key_perm, N_ROW * N_COL)
    orders = jax.vmap(lambda single: jax.random.permutation(single, total_slots))(perm_keys)
    orders = orders.reshape(N_ROW, N_COL, N_ROW, CAPB)
    rates = jax.random.randint(key_rate, (N_ROW, N_COL, 1, 1), 35, 101)
    chosen = jax.random.randint(key_full, (1, N_COL, 1, 1), 0, N_ROW)
    rolls = jax.random.randint(key_roll, (N_ROW, N_COL, N_ROW, CAPB), 0, 100)
    target = jnp.arange(N_ROW).reshape(N_ROW, 1, 1, 1)
    grid_cols = jnp.arange(N_COL).reshape(1, N_COL, 1, 1)
    is_live = (orders < NPOS) & ((rolls < rates) | (target == chosen))
    local_row = orders // NC
    local_col = orders % NC
    panel_index = (target + grid_cols) % N_ROW
    block_row = jnp.where(is_live, panel_index * MB + local_row, -1)
    block_col = jnp.where(is_live, grid_cols * NC + local_col, -1)
    stacked = jnp.stack([block_row, block_col], axis=-1)
    return stacked.transpose(2, 1, 0, 3, 4).reshape(N_ROW, N_COL, N_ROW * CAPB, 2).astype(jnp.int32)


def set_ends(array, stream_key, least, high):
    longest = array.shape.index(max(array.shape))
    spots = []
    for shift in (0, 1):
        where = [jax.random.randint(jax.random.fold_in(stream_key, axis), (), 0, length) for axis, length in enumerate(array.shape)]
        where[longest] = (where[longest] + shift) % array.shape[longest]
        spots.append(tuple(where))
    return array.at[spots[0]].set(least).at[spots[1]].set(high)


def steps_of(stream_key, dims, cuts, low, high):
    loudness, own = 1.0, jax.random.fold_in(stream_key, 6)
    for axis_at, parts in cuts:
        steps = jnp.exp(jax.random.uniform(jax.random.fold_in(own, axis_at), (parts,), jnp.float32, low / len(cuts), high / len(cuts)))
        loudness = loudness * jnp.repeat(steps, dims[axis_at] // parts).reshape([-1 if axis == axis_at else 1 for axis in range(len(dims))])
    return loudness


def bell_draw(rng, extent, scale, limit, pieces=(), kind=jnp.bfloat16):
    result = jax.random.normal(rng, extent, jnp.float32) * scale
    if len(pieces) > 0:
        result = steps_of(rng, extent, pieces, -0.22, 0.18) * result
    return jnp.clip(result, min=-limit, max=limit).astype(kind)


def setup_inputs(seed: int = 0) -> dict:
    streams_of = jax.random.split(jax.random.key(seed), 6)
    return {
        "a_blocks": bell_draw(streams_of[0], (N_ROW, N_COL, SLOTS_A, BS, BS), 1.0, 6.0, ((0, 8), (1, 4))),
        "a_coord": draw_a_coord(jax.random.fold_in(streams_of[5], 71), 0),
        "b_blocks": bell_draw(streams_of[2], (N_ROW, N_COL, SLOTS_B, BS, BS), (NB * BS // 2) ** -0.5, 0.125, ((0, 8), (1, 4))),
        "b_coord": draw_b_coord(jax.random.fold_in(streams_of[5], 71), 0),
        "c_mask": set_ends((jax.random.randint(streams_of[4], (NB, NB), 0, 3) < 2).astype(jnp.int32), jax.random.fold_in(streams_of[4], 1), 0, 1),
    }


def assemble(blocks, coords):
    flat_blocks = blocks.reshape(-1, BS, BS)
    coord_list = coords.reshape(-1, 2)
    is_live = coord_list[:, 0] >= 0
    target = jnp.where(is_live, coord_list[:, 0] * NB + coord_list[:, 1], NB * NB).astype(jnp.int32)
    dense_blocks = jnp.zeros((NB * NB, BS, BS), blocks.dtype).at[target].set(flat_blocks, mode="drop")
    return dense_blocks.reshape(NB, NB, BS, BS).transpose(0, 2, 1, 3).reshape(NB * BS, NB * BS)


def reference(a_blocks, a_coord, b_blocks, b_coord, c_mask):
    left_matrix = assemble(a_blocks, a_coord)
    right_matrix = assemble(b_blocks, b_coord)
    product = jnp.dot(left_matrix, right_matrix, preferred_element_type=jnp.float32)
    masked = product.reshape(NB, BS, NB, BS) * c_mask[:, None, :, None].astype(jnp.float32)
    return masked.reshape(NB * BS, NB * BS)
```

```python
import functools

import jax
import jax.numpy as jnp
from jax import lax
from jax.experimental import pallas as pl
from jax.experimental.pallas import tpu as pltpu
from jax.sharding import PartitionSpec as P

MESH = pl.DeviceIdType.MESH
AHEAD = 3


def kernel(
    rows, cols, slots, band_rows, band_cols,
    a_ref, b_ref, code_a_ref, code_b_ref, o_ref, *scratch,
):
    panels = rows
    chips = rows // 2
    cap_a, cap_b = slots // cols, slots // rows
    ratio = panels // cols
    nb = panels * band_rows
    bs = a_ref.shape[-1]
    buf_a = scratch[:cols]
    buf_b = scratch[cols : cols + panels]
    (
        tile_a, tile_b, codes_a, codes_b, inv_v, inv_s,
        own_a_sem, own_b_sem, a_send, a_recv, ca_send, ca_recv, cb_send, cb_recv,
        up_send, down_send, z_recv, sib_send, sib_recv, local_sem,
    ) = scratch[cols + panels :]

    r = lax.axis_index("row")
    c = lax.axis_index("col")
    z = r // 2
    core = r % 2
    sibling = z * 2 + (1 - core)

    barrier = pltpu.get_barrier_semaphore()
    for off in range(1, cols):
        pl.semaphore_signal(barrier, inc=1, device_id=(r, (c + off) % cols), device_id_type=MESH)
    for off in range(1, rows):
        pl.semaphore_signal(barrier, inc=1, device_id=((r + off) % rows, c), device_id_type=MESH)

    order = [s + m * cols for s in range(cols) for m in range(ratio)]

    def own_a(s):
        group = (s - r % cols + cols) % cols
        return pltpu.make_async_copy(
            a_ref.at[pl.ds(group * cap_a, cap_a)],
            buf_a[s].at[pl.ds(1 + c * cap_a, cap_a)], own_a_sem.at[s])

    def send_a(s, off):
        group = (s - r % cols + cols) % cols
        return pltpu.make_async_remote_copy(
            src_ref=a_ref.at[pl.ds(group * cap_a, cap_a)],
            dst_ref=buf_a[s].at[pl.ds(1 + c * cap_a, cap_a)],
            send_sem=a_send.at[s, off - 1], recv_sem=a_recv.at[s, off - 1],
            device_id=(r, (c + off) % cols), device_id_type=MESH)

    def take_a(s, off):
        source = (c - off + cols) % cols
        return pltpu.make_async_remote_copy(
            src_ref=a_ref.at[pl.ds(0, cap_a)],
            dst_ref=buf_a[s].at[pl.ds(1 + source * cap_a, cap_a)],
            send_sem=a_send.at[s, off - 1], recv_sem=a_recv.at[s, off - 1],
            device_id=(r, (c + off) % cols), device_id_type=MESH)

    def own_slots(p):
        group = (p - c + panels) % panels
        return b_ref.at[pl.ds(group * cap_b, cap_b)]

    def place(p, owner_row):
        return buf_b[p].at[pl.ds(1 + owner_row * cap_b, cap_b)]

    def own_b(p):
        return pltpu.make_async_copy(own_slots(p), place(p, r), own_b_sem.at[p])

    def along(p, chip, up, own):
        owner = chip * 2 + core
        step = 2 if up else -2
        return pltpu.make_async_remote_copy(
            src_ref=own_slots(p) if own else place(p, owner), dst_ref=place(p, owner),
            send_sem=(up_send if up else down_send).at[p, chip], recv_sem=z_recv.at[p, chip],
            device_id=(r + step, c), device_id_type=MESH)

    def across(p, chip, own):
        owner = chip * 2 + core
        return pltpu.make_async_remote_copy(
            src_ref=own_slots(p) if own else place(p, owner), dst_ref=place(p, owner),
            send_sem=sib_send.at[p, chip], recv_sem=sib_recv.at[p, chip],
            device_id=(sibling, c), device_id_type=MESH)

    def take_across(p, chip):
        owner = chip * 2 + (1 - core)
        return pltpu.make_async_remote_copy(
            src_ref=place(p, owner), dst_ref=place(p, owner),
            send_sem=sib_send.at[p, chip], recv_sem=sib_recv.at[p, chip],
            device_id=(sibling, c), device_id_type=MESH)

    def code_a(off, source):
        return pltpu.make_async_remote_copy(
            src_ref=code_a_ref, dst_ref=codes_a.at[pl.ds(source * slots, slots)],
            send_sem=ca_send.at[off - 1], recv_sem=ca_recv.at[off - 1],
            device_id=(r, (c + off) % cols), device_id_type=MESH)

    def code_b(off, source):
        return pltpu.make_async_remote_copy(
            src_ref=code_b_ref, dst_ref=codes_b.at[pl.ds(source * slots, slots)],
            send_sem=cb_send.at[off - 1], recv_sem=cb_recv.at[off - 1],
            device_id=((r + off) % rows, c), device_id_type=MESH)

    def start_own_b(p):
        @pl.when(z > 0)
        def _():
            along(p, z, False, True).start()

        @pl.when(z < chips - 1)
        def _():
            along(p, z, True, True).start()

        across(p, z, True).start()

    def start_a(s):
        for off in range(1, cols):
            send_a(s, off).start()

    pl.semaphore_wait(barrier, rows + cols - 2)
    start_own_b(order[0])
    start_a(0)
    for off in range(1, cols):
        code_a(off, c).start()
    for off in range(1, rows):
        code_b(off, r).start()
    for k in range(1, min(AHEAD, panels)):
        start_own_b(order[k])
    if cols > 1:
        start_a(1)
    for s in range(cols):
        own_a(s).start()
    for p in order:
        own_b(p).start()
    codes_a[pl.ds(c * slots, slots), :] = code_a_ref[...]
    codes_b[pl.ds(r * slots, slots), :] = code_b_ref[...]
    for ref in buf_a + buf_b:
        ref[0] = jnp.zeros((bs, bs), ref.dtype)

    def inverse(codes, cap, keys, first_row):
        count = codes.shape[0]
        number = lax.broadcasted_iota(jnp.int32, (count, 128), 0)
        ident = (number // slots) * cap + number % cap + 1
        lane = lax.broadcasted_iota(jnp.int32, (count, 128), 1)
        for part in range(keys // 128):
            hit = codes[...] == lane + part * 128
            inv_v[pl.ds(first_row + part, 1), :] = jnp.max(
                jnp.where(hit, ident, 0), axis=0, keepdims=True)

    keys_a, keys_b = band_rows * nb, nb * band_cols
    rows_a = keys_a // 128

    def panel_traffic(p):
        for d in range(1, chips):
            @pl.when(z - d >= 0)
            def _():
                along(p, z - d, True, False).wait_recv()

                @pl.when(z < chips - 1)
                def _():
                    along(p, z - d, True, False).start()

                across(p, z - d, False).start()

            @pl.when(z + d < chips)
            def _():
                along(p, z + d, False, False).wait_recv()

                @pl.when(z > 0)
                def _():
                    along(p, z + d, False, False).start()

                across(p, z + d, False).start()

    for k, p in enumerate(order):
        s = p % cols
        if k + AHEAD < panels:
            start_own_b(order[k + AHEAD])
        if k % ratio == 0 and s + 2 < cols:
            start_a(s + 2)
        if k == 0:
            for off in range(1, cols):
                code_a(off, (c - off + cols) % cols).wait_recv()
            for off in range(1, rows):
                code_b(off, (r - off + rows) % rows).wait_recv()
            inverse(codes_a, cap_a, keys_a, 0)
            inverse(codes_b, cap_b, keys_b, rows_a)
            move = pltpu.make_async_copy(inv_v, inv_s, local_sem)
            move.start()
            move.wait()
        panel_traffic(p)
        if k % ratio == 0:
            own_a(s).wait()
            for off in range(1, cols):
                take_a(s, off).wait_recv()
        own_b(p).wait()
        for chip in range(chips):
            take_across(p, chip).wait_recv()

        def spot(key, first_row):
            return inv_s[first_row + key // 128, key % 128]

        for lr in range(band_rows):
            for lk in range(band_rows):
                at = spot(lr * nb + p * band_rows + lk, 0)
                tile_a[lr * bs : (lr + 1) * bs, lk * bs : (lk + 1) * bs] = buf_a[s][at]
        for lk in range(band_rows):
            for lc in range(band_cols):
                at = spot((p * band_rows + lk) * band_cols + lc, rows_a)
                tile_b[lk * bs : (lk + 1) * bs, lc * bs : (lc + 1) * bs] = buf_b[p][at]

        def columns(n, carry):
            where = pl.ds(pl.multiple_of(n * 256, 256), 256)
            part = jnp.dot(tile_a[...], tile_b[:, where], preferred_element_type=jnp.float32)
            if k == 0:
                o_ref[:, where] = part
            else:
                o_ref[:, where] += part
            return carry

        lax.fori_loop(0, band_cols * bs // 256, columns, 0)

    for off in range(1, cols):
        code_a(off, c).wait_send()
        for s in range(cols):
            send_a(s, off).wait_send()
    for off in range(1, rows):
        code_b(off, r).wait_send()
    for p in order:
        for chip in range(chips):
            across(p, chip, False).wait_send()

            @pl.when((z < chips - 1) & (chip <= z))
            def _():
                along(p, chip, True, False).wait_send()

            @pl.when((z > 0) & (chip >= z))
            def _():
                along(p, chip, False, False).wait_send()


def shards(a_blocks, a_coord, b_blocks, b_coord, c_mask):
    rows = lax.axis_size("row")
    cols = lax.axis_size("col")
    slots, bs = a_blocks.shape[2], a_blocks.shape[-1]
    band_rows, band_cols = c_mask.shape
    chips = rows // 2
    nb = rows * band_rows
    a_tags = a_coord.reshape(slots, 2)
    b_tags = b_coord.reshape(slots, 2)
    code_a = jnp.where(
        a_tags[:, 0] >= 0,
        (a_tags[:, 0] - lax.axis_index("row") * band_rows) * nb + a_tags[:, 1], -1)
    code_b = jnp.where(
        b_tags[:, 0] >= 0,
        b_tags[:, 0] * band_cols + b_tags[:, 1] - lax.axis_index("col") * band_cols, -1)
    code_a = jnp.broadcast_to(code_a[:, None], (slots, 128))
    code_b = jnp.broadcast_to(code_b[:, None], (slots, 128))
    inv_rows = (band_rows * nb + nb * band_cols) // 128
    inv_rows = (inv_rows + 7) // 8 * 8
    dma = pltpu.SemaphoreType.DMA
    wide, tall = band_cols * bs, band_rows * bs
    product = pl.pallas_call(
        functools.partial(kernel, rows, cols, slots, band_rows, band_cols),
        out_shape=jax.ShapeDtypeStruct((tall, wide), jnp.float32),
        in_specs=[
            pl.BlockSpec(memory_space=pl.ANY),
            pl.BlockSpec(memory_space=pl.ANY),
            pl.BlockSpec(memory_space=pltpu.VMEM),
            pl.BlockSpec(memory_space=pltpu.VMEM),
        ],
        out_specs=pl.BlockSpec(memory_space=pltpu.VMEM),
        scratch_shapes=(
            [pltpu.VMEM((1 + slots, bs, bs), jnp.bfloat16)] * cols
            + [pltpu.VMEM((1 + slots, bs, bs), jnp.bfloat16)] * rows
            + [
                pltpu.VMEM((tall, tall), jnp.bfloat16),
                pltpu.VMEM((tall, wide), jnp.bfloat16),
                pltpu.VMEM((cols * slots, 128), jnp.int32),
                pltpu.VMEM((rows * slots, 128), jnp.int32),
                pltpu.VMEM((inv_rows, 128), jnp.int32),
                pltpu.SMEM((inv_rows, 128), jnp.int32),
                dma((cols,)), dma((rows,)),
                dma((cols, cols - 1)), dma((cols, cols - 1)),
                dma((cols - 1,)), dma((cols - 1,)),
                dma((rows - 1,)), dma((rows - 1,)),
                dma((rows, chips)), dma((rows, chips)), dma((rows, chips)),
                dma((rows, chips)), dma((rows, chips)),
                dma,
            ]
        ),
        compiler_params=pltpu.CompilerParams(
            collective_id=0, has_side_effects=True, vmem_limit_bytes=52 * 2**20),
        cost_estimate=pl.CostEstimate(
            flops=2 * tall * wide * nb * bs, transcendentals=0,
            bytes_accessed=(cols + rows) * slots * bs * bs * 2 + tall * wide * 4),
    )(a_blocks.reshape(slots, bs, bs), b_blocks.reshape(slots, bs, bs), code_a, code_b)
    masked = product.reshape(band_rows, bs, band_cols, bs) * c_mask[:, None, :, None].astype(
        jnp.float32)
    return masked.reshape(tall, wide)


def solution(mesh):
    placed = (
        P("row", "col", None, None, None),
        P("row", "col", None, None),
        P("row", "col", None, None, None),
        P("row", "col", None, None),
        P("row", "col"),
    )
    return jax.shard_map(
        shards, mesh=mesh, in_specs=placed, out_specs=P("row", "col"), check_vma=False
    )
```

```python
import functools

import jax
import jax.numpy as jnp
from jax import lax
from jax.experimental import pallas as pl
from jax.experimental.pallas import tpu as pltpu
from jax.sharding import PartitionSpec as P

MESH = pl.DeviceIdType.MESH
AHEAD = 3


def kernel(
    rows, cols, slots, band_rows, band_cols,
    a_ref, b_ref, tags_a_ref, tags_b_ref, mask_ref, o_ref, *scratch,
):
    panels = rows
    chips = rows // 2
    cap_a, cap_b = slots // cols, slots // rows
    ratio = panels // cols
    nb = panels * band_rows
    bs = a_ref.shape[-1]
    buf_a = scratch[:cols]
    buf_b = scratch[cols : cols + panels]
    (
        tile_a, tile_b, code_a_ref, code_b_ref, codes_a, codes_b, inv_v, inv_s,
        own_a_sem, own_b_sem, a_send, a_recv, ca_send, ca_recv, cb_send, cb_recv,
        up_send, down_send, z_recv, sib_send, sib_recv, local_sem,
    ) = scratch[cols + panels :]

    r = lax.axis_index("row")
    c = lax.axis_index("col")
    z = r // 2
    core = r % 2
    sibling = z * 2 + (1 - core)

    barrier = pltpu.get_barrier_semaphore()
    for off in range(1, cols):
        pl.semaphore_signal(barrier, inc=1, device_id=(r, (c + off) % cols), device_id_type=MESH)
    for off in range(1, rows):
        pl.semaphore_signal(barrier, inc=1, device_id=((r + off) % rows, c), device_id_type=MESH)

    order = [s + m * cols for s in range(cols) for m in range(ratio)]

    def own_a(s):
        group = (s - r % cols + cols) % cols
        return pltpu.make_async_copy(
            a_ref.at[pl.ds(group * cap_a, cap_a)],
            buf_a[s].at[pl.ds(1 + c * cap_a, cap_a)], own_a_sem.at[s])

    def send_a(s, off):
        group = (s - r % cols + cols) % cols
        return pltpu.make_async_remote_copy(
            src_ref=a_ref.at[pl.ds(group * cap_a, cap_a)],
            dst_ref=buf_a[s].at[pl.ds(1 + c * cap_a, cap_a)],
            send_sem=a_send.at[s, off - 1], recv_sem=a_recv.at[s, off - 1],
            device_id=(r, (c + off) % cols), device_id_type=MESH)

    def take_a(s, off):
        source = (c - off + cols) % cols
        return pltpu.make_async_remote_copy(
            src_ref=a_ref.at[pl.ds(0, cap_a)],
            dst_ref=buf_a[s].at[pl.ds(1 + source * cap_a, cap_a)],
            send_sem=a_send.at[s, off - 1], recv_sem=a_recv.at[s, off - 1],
            device_id=(r, (c + off) % cols), device_id_type=MESH)

    def own_slots(p):
        group = (p - c + panels) % panels
        return b_ref.at[pl.ds(group * cap_b, cap_b)]

    def place(p, owner_row):
        return buf_b[p].at[pl.ds(1 + owner_row * cap_b, cap_b)]

    def own_b(p):
        return pltpu.make_async_copy(own_slots(p), place(p, r), own_b_sem.at[p])

    def along(p, chip, up, own):
        owner = chip * 2 + core
        step = 2 if up else -2
        return pltpu.make_async_remote_copy(
            src_ref=own_slots(p) if own else place(p, owner), dst_ref=place(p, owner),
            send_sem=(up_send if up else down_send).at[p, chip], recv_sem=z_recv.at[p, chip],
            device_id=(r + step, c), device_id_type=MESH)

    def across(p, chip, own):
        owner = chip * 2 + core
        return pltpu.make_async_remote_copy(
            src_ref=own_slots(p) if own else place(p, owner), dst_ref=place(p, owner),
            send_sem=sib_send.at[p, chip], recv_sem=sib_recv.at[p, chip],
            device_id=(sibling, c), device_id_type=MESH)

    def take_across(p, chip):
        owner = chip * 2 + (1 - core)
        return pltpu.make_async_remote_copy(
            src_ref=place(p, owner), dst_ref=place(p, owner),
            send_sem=sib_send.at[p, chip], recv_sem=sib_recv.at[p, chip],
            device_id=(sibling, c), device_id_type=MESH)

    def code_a(off, source):
        return pltpu.make_async_remote_copy(
            src_ref=code_a_ref, dst_ref=codes_a.at[pl.ds(source * 8, 8)],
            send_sem=ca_send.at[off - 1], recv_sem=ca_recv.at[off - 1],
            device_id=(r, (c + off) % cols), device_id_type=MESH)

    def code_b(off, source):
        return pltpu.make_async_remote_copy(
            src_ref=code_b_ref, dst_ref=codes_b.at[pl.ds(source * 8, 8)],
            send_sem=cb_send.at[off - 1], recv_sem=cb_recv.at[off - 1],
            device_id=((r + off) % rows, c), device_id_type=MESH)

    def start_own_b(p):
        @pl.when(z > 0)
        def _():
            along(p, z, False, True).start()

        @pl.when(z < chips - 1)
        def _():
            along(p, z, True, True).start()

        across(p, z, True).start()

    def start_a(s):
        for off in range(1, cols):
            send_a(s, off).start()

    def note(tags, code_ref, across_part, down_part):
        code = jnp.where(tags[0:1, :] >= 0, across_part(tags[0:1, :]) + down_part(tags[1:2, :]), -1)
        code_ref[...] = jnp.full((8, 128), -1, jnp.int32)
        code_ref[:, :slots] = jnp.broadcast_to(code, (8, slots))

    note(tags_a_ref, code_a_ref, lambda x: (x - r * band_rows) * nb, lambda x: x)
    note(tags_b_ref, code_b_ref, lambda x: x * band_cols, lambda x: x - c * band_cols)
    pl.semaphore_wait(barrier, rows + cols - 2)
    start_own_b(order[0])
    start_a(0)
    for off in range(1, cols):
        code_a(off, c).start()
    for off in range(1, rows):
        code_b(off, r).start()
    for k in range(1, min(AHEAD, panels)):
        start_own_b(order[k])
    if cols > 1:
        start_a(1)
    for s in range(cols):
        own_a(s).start()
    for p in order:
        own_b(p).start()
    codes_a[pl.ds(pl.multiple_of(c * 8, 8), 8), :] = code_a_ref[...]
    codes_b[pl.ds(pl.multiple_of(r * 8, 8), 8), :] = code_b_ref[...]
    for ref in buf_a + buf_b:
        ref[0] = jnp.zeros((bs, bs), ref.dtype)

    def inverse(codes, cap, keys, first_row):
        number = lax.broadcasted_iota(jnp.int32, (slots, 128), 0)
        lane = lax.broadcasted_iota(jnp.int32, (slots, 128), 1)
        found = [jnp.zeros((slots, 128), jnp.int32) for _ in range(keys // 128)]
        for source in range(codes.shape[0] // 8):
            row = codes[source * 8 : source * 8 + 1, :]
            column = jnp.broadcast_to(row, (128, 128)).T[:slots, :]
            ident = source * cap + number % cap + 1
            for part in range(keys // 128):
                found[part] = jnp.where(column == lane + part * 128, ident, found[part])
        for part in range(keys // 128):
            inv_v[first_row + part : first_row + part + 1, :] = jnp.max(
                found[part], axis=0, keepdims=True)

    keys_a, keys_b = band_rows * nb, nb * band_cols
    rows_a = keys_a // 128

    def hop(p, d):
        @pl.when(z - d >= 0)
        def _():
            along(p, z - d, True, False).wait_recv()

            @pl.when(z < chips - 1)
            def _():
                along(p, z - d, True, False).start()

            across(p, z - d, False).start()

        @pl.when(z + d < chips)
        def _():
            along(p, z + d, False, False).wait_recv()

            @pl.when(z > 0)
            def _():
                along(p, z + d, False, False).start()

            across(p, z + d, False).start()

    def spot(key, first_row):
        return inv_s[first_row + key // 128, key % 128]

    def gather_a(k):
        p = order[k]
        s = p % cols
        if k == 0:
            for off in range(1, cols):
                code_a(off, (c - off + cols) % cols).wait_recv()
            for off in range(1, rows):
                code_b(off, (r - off + rows) % rows).wait_recv()
            inverse(codes_a, cap_a, keys_a, 0)
            inverse(codes_b, cap_b, keys_b, rows_a)
            move = pltpu.make_async_copy(inv_v, inv_s, local_sem)
            move.start()
            move.wait()
        if k % ratio == 0:
            own_a(s).wait()
            for off in range(1, cols):
                take_a(s, off).wait_recv()
        for lr in range(band_rows):
            for lk in range(band_rows):
                at = spot(lr * nb + p * band_rows + lk, 0)
                tile_a[lr * bs : (lr + 1) * bs, lk * bs : (lk + 1) * bs] = buf_a[s][at]
        own_b(p).wait()
        for chip in range(chips):
            take_across(p, chip).wait_recv()

    pair = 2 * bs

    def columns(k, n):
        p = order[k]
        for lk in range(band_rows):
            for half in range(2):
                at = spot((p * band_rows + lk) * band_cols + n * 2 + half, rows_a)
                tile_b[lk * bs : (lk + 1) * bs, half * bs : (half + 1) * bs] = buf_b[p][at]
        part = jnp.dot(tile_a[...], tile_b[...], preferred_element_type=jnp.float32)
        where = slice(n * pair, (n + 1) * pair)
        if k > 0:
            part = o_ref[:, where] + part
        if k < panels - 1:
            o_ref[:, where] = part
        else:
            for lr in range(band_rows):
                for half in range(2):
                    lc = n * 2 + half
                    o_ref[lr * bs : (lr + 1) * bs, lc * bs : (lc + 1) * bs] = part[
                        lr * bs : (lr + 1) * bs, half * bs : (half + 1) * bs
                    ] * mask_ref[lr, lc].astype(jnp.float32)

    def work(k):
        parts = [functools.partial(gather_a, k)]
        return parts + [functools.partial(columns, k, n) for n in range(band_cols // 2)]

    for k, p in enumerate(order):
        s = p % cols
        if k + AHEAD < panels:
            start_own_b(order[k + AHEAD])
        if k % ratio == 0 and s + 2 < cols:
            start_a(s + 2)
        parts = work(k - 1) if k > 0 else []
        share = -(-len(parts) // (chips - 1))
        for d in range(1, chips):
            hop(p, d)
            for part in parts[(d - 1) * share : d * share]:
                part()
    for part in work(panels - 1):
        part()

    for off in range(1, cols):
        code_a(off, c).wait_send()
        for s in range(cols):
            send_a(s, off).wait_send()
    for off in range(1, rows):
        code_b(off, r).wait_send()
    for p in order:
        for chip in range(chips):
            across(p, chip, False).wait_send()

            @pl.when((z < chips - 1) & (chip <= z))
            def _():
                along(p, chip, True, False).wait_send()

            @pl.when((z > 0) & (chip >= z))
            def _():
                along(p, chip, False, False).wait_send()


def shards(a_blocks, a_coord, b_blocks, b_coord, c_mask):
    rows = lax.axis_size("row")
    cols = lax.axis_size("col")
    slots, bs = a_blocks.shape[2], a_blocks.shape[-1]
    band_rows, band_cols = c_mask.shape
    chips = rows // 2
    nb = rows * band_rows
    a_tags = a_coord.reshape(slots, 2).T
    b_tags = b_coord.reshape(slots, 2).T
    inv_rows = (band_rows * nb + nb * band_cols) // 128
    inv_rows = (inv_rows + 7) // 8 * 8
    dma = pltpu.SemaphoreType.DMA
    wide, tall = band_cols * bs, band_rows * bs
    return pl.pallas_call(
        functools.partial(kernel, rows, cols, slots, band_rows, band_cols),
        out_shape=jax.ShapeDtypeStruct((tall, wide), jnp.float32),
        in_specs=[
            pl.BlockSpec(memory_space=pl.ANY),
            pl.BlockSpec(memory_space=pl.ANY),
            pl.BlockSpec(memory_space=pltpu.VMEM),
            pl.BlockSpec(memory_space=pltpu.VMEM),
            pl.BlockSpec(memory_space=pltpu.SMEM),
        ],
        out_specs=pl.BlockSpec(memory_space=pltpu.VMEM),
        scratch_shapes=(
            [pltpu.VMEM((1 + slots, bs, bs), jnp.bfloat16)] * cols
            + [pltpu.VMEM((1 + slots, bs, bs), jnp.bfloat16)] * rows
            + [
                pltpu.VMEM((tall, tall), jnp.bfloat16),
                pltpu.VMEM((tall, 2 * bs), jnp.bfloat16),
                pltpu.VMEM((8, 128), jnp.int32),
                pltpu.VMEM((8, 128), jnp.int32),
                pltpu.VMEM((cols * 8, 128), jnp.int32),
                pltpu.VMEM((rows * 8, 128), jnp.int32),
                pltpu.VMEM((inv_rows, 128), jnp.int32),
                pltpu.SMEM((inv_rows, 128), jnp.int32),
                dma((cols,)), dma((rows,)),
                dma((cols, cols - 1)), dma((cols, cols - 1)),
                dma((cols - 1,)), dma((cols - 1,)),
                dma((rows - 1,)), dma((rows - 1,)),
                dma((rows, chips)), dma((rows, chips)), dma((rows, chips)),
                dma((rows, chips)), dma((rows, chips)),
                dma,
            ]
        ),
        compiler_params=pltpu.CompilerParams(
            collective_id=0, has_side_effects=True, vmem_limit_bytes=62 * 2**20),
        cost_estimate=pl.CostEstimate(
            flops=2 * tall * wide * nb * bs, transcendentals=0,
            bytes_accessed=(cols + rows) * slots * bs * bs * 2 + tall * wide * 4),
    )(a_blocks.reshape(slots, bs, bs), b_blocks.reshape(slots, bs, bs), a_tags, b_tags, c_mask)


def solution(mesh):
    placed = (
        P("row", "col", None, None, None),
        P("row", "col", None, None),
        P("row", "col", None, None, None),
        P("row", "col", None, None),
        P("row", "col"),
    )
    return jax.shard_map(
        shards, mesh=mesh, in_specs=placed, out_specs=P("row", "col"), check_vma=False
    )
```

```python
import functools

import jax
import jax.numpy as jnp
from jax import lax
from jax.experimental import pallas as pl
from jax.experimental.pallas import tpu as pltpu
from jax.sharding import PartitionSpec as P

MESH = pl.DeviceIdType.MESH
AHEAD = 3


def kernel(
    rows, cols, slots, band_rows, band_cols,
    a_ref, b_ref, tags_a_ref, tags_b_ref, mask_ref, out_ref, *scratch,
):
    panels = rows
    chips = rows // 2
    cap_a, cap_b = slots // cols, slots // rows
    ratio = panels // cols
    nb = panels * band_rows
    bs = a_ref.shape[-1]
    buf_a = scratch[:cols]
    buf_b = scratch[cols : cols + panels]
    (
        o_ref, out_sem, tiles_a, tile_b, code_a_ref, code_b_ref, codes_a, codes_b, inv_v, inv_s,
        own_a_sem, own_b_sem, a_send, a_recv, ca_send, ca_recv, cb_send, cb_recv,
        up_send, down_send, z_recv, sib_send, sib_recv, local_sem,
    ) = scratch[cols + panels :]

    r = lax.axis_index("row")
    c = lax.axis_index("col")
    z = r // 2
    core = r % 2
    sibling = z * 2 + (1 - core)

    barrier = pltpu.get_barrier_semaphore()
    for off in range(1, cols):
        pl.semaphore_signal(barrier, inc=1, device_id=(r, (c + off) % cols), device_id_type=MESH)
    for off in range(1, rows):
        pl.semaphore_signal(barrier, inc=1, device_id=((r + off) % rows, c), device_id_type=MESH)

    order = [s + m * cols for s in range(cols) for m in range(ratio)]

    def own_a(s):
        group = (s - r % cols + cols) % cols
        return pltpu.make_async_copy(
            a_ref.at[pl.ds(group * cap_a, cap_a)],
            buf_a[s].at[pl.ds(1 + c * cap_a, cap_a)], own_a_sem.at[s])

    def send_a(s, off):
        group = (s - r % cols + cols) % cols
        return pltpu.make_async_remote_copy(
            src_ref=a_ref.at[pl.ds(group * cap_a, cap_a)],
            dst_ref=buf_a[s].at[pl.ds(1 + c * cap_a, cap_a)],
            send_sem=a_send.at[s, off - 1], recv_sem=a_recv.at[s, off - 1],
            device_id=(r, (c + off) % cols), device_id_type=MESH)

    def take_a(s, off):
        source = (c - off + cols) % cols
        return pltpu.make_async_remote_copy(
            src_ref=a_ref.at[pl.ds(0, cap_a)],
            dst_ref=buf_a[s].at[pl.ds(1 + source * cap_a, cap_a)],
            send_sem=a_send.at[s, off - 1], recv_sem=a_recv.at[s, off - 1],
            device_id=(r, (c + off) % cols), device_id_type=MESH)

    def own_slots(p):
        group = (p - c + panels) % panels
        return b_ref.at[pl.ds(group * cap_b, cap_b)]

    def place(p, owner_row):
        return buf_b[p].at[pl.ds(1 + owner_row * cap_b, cap_b)]

    def own_b(p):
        return pltpu.make_async_copy(own_slots(p), place(p, r), own_b_sem.at[p])

    def along(p, chip, up, own):
        owner = chip * 2 + core
        step = 2 if up else -2
        return pltpu.make_async_remote_copy(
            src_ref=own_slots(p) if own else place(p, owner), dst_ref=place(p, owner),
            send_sem=(up_send if up else down_send).at[p, chip], recv_sem=z_recv.at[p, chip],
            device_id=(r + step, c), device_id_type=MESH)

    def across(p, chip, own):
        owner = chip * 2 + core
        return pltpu.make_async_remote_copy(
            src_ref=own_slots(p) if own else place(p, owner), dst_ref=place(p, owner),
            send_sem=sib_send.at[p, chip], recv_sem=sib_recv.at[p, chip],
            device_id=(sibling, c), device_id_type=MESH)

    def take_across(p, chip):
        owner = chip * 2 + (1 - core)
        return pltpu.make_async_remote_copy(
            src_ref=place(p, owner), dst_ref=place(p, owner),
            send_sem=sib_send.at[p, chip], recv_sem=sib_recv.at[p, chip],
            device_id=(sibling, c), device_id_type=MESH)

    def code_a(off, source):
        return pltpu.make_async_remote_copy(
            src_ref=code_a_ref, dst_ref=codes_a.at[pl.ds(source * 8, 8)],
            send_sem=ca_send.at[off - 1], recv_sem=ca_recv.at[off - 1],
            device_id=(r, (c + off) % cols), device_id_type=MESH)

    def code_b(off, source):
        return pltpu.make_async_remote_copy(
            src_ref=code_b_ref, dst_ref=codes_b.at[pl.ds(source * 8, 8)],
            send_sem=cb_send.at[off - 1], recv_sem=cb_recv.at[off - 1],
            device_id=((r + off) % rows, c), device_id_type=MESH)

    def start_own_b(p):
        @pl.when(z > 0)
        def _():
            along(p, z, False, True).start()

        @pl.when(z < chips - 1)
        def _():
            along(p, z, True, True).start()

        across(p, z, True).start()

    def start_a(s):
        for off in range(1, cols):
            send_a(s, off).start()

    def note(tags, code_ref, across_part, down_part):
        code = jnp.where(tags[0:1, :] >= 0, across_part(tags[0:1, :]) + down_part(tags[1:2, :]), -1)
        code_ref[...] = jnp.full((8, 128), -1, jnp.int32)
        code_ref[:, :slots] = jnp.broadcast_to(code, (8, slots))

    note(tags_a_ref, code_a_ref, lambda x: (x - r * band_rows) * nb, lambda x: x)
    note(tags_b_ref, code_b_ref, lambda x: x * band_cols, lambda x: x - c * band_cols)
    pl.semaphore_wait(barrier, rows + cols - 2)
    start_own_b(order[0])
    start_a(0)
    for off in range(1, cols):
        code_a(off, c).start()
    for off in range(1, rows):
        code_b(off, r).start()
    for k in range(1, min(AHEAD, panels)):
        start_own_b(order[k])
    if cols > 1:
        start_a(1)
    for s in range(cols):
        own_a(s).start()
    for p in order:
        own_b(p).start()
    codes_a[pl.ds(pl.multiple_of(c * 8, 8), 8), :] = code_a_ref[...]
    codes_b[pl.ds(pl.multiple_of(r * 8, 8), 8), :] = code_b_ref[...]
    for ref in buf_a + buf_b:
        ref[0] = jnp.zeros((bs, bs), ref.dtype)

    def inverse(codes, cap, keys, first_row):
        number = lax.broadcasted_iota(jnp.int32, (slots, 128), 0)
        lane = lax.broadcasted_iota(jnp.int32, (slots, 128), 1)
        found = [jnp.zeros((slots, 128), jnp.int32) for _ in range(keys // 128)]
        for source in range(codes.shape[0] // 8):
            row = codes[source * 8 : source * 8 + 1, :]
            column = jnp.broadcast_to(row, (128, 128)).T[:slots, :]
            ident = source * cap + number % cap + 1
            for part in range(keys // 128):
                found[part] = jnp.where(column == lane + part * 128, ident, found[part])
        for part in range(keys // 128):
            inv_v[first_row + part : first_row + part + 1, :] = jnp.max(
                found[part], axis=0, keepdims=True)

    keys_a, keys_b = band_rows * nb, nb * band_cols
    rows_a = keys_a // 128

    def hop(p, d):
        @pl.when(z - d >= 0)
        def _():
            along(p, z - d, True, False).wait_recv()

            @pl.when(z < chips - 1)
            def _():
                along(p, z - d, True, False).start()

            across(p, z - d, False).start()

        @pl.when(z + d < chips)
        def _():
            along(p, z + d, False, False).wait_recv()

            @pl.when(z > 0)
            def _():
                along(p, z + d, False, False).start()

            across(p, z + d, False).start()

    def spot(key, first_row):
        return inv_s[first_row + key // 128, key % 128]

    def gather_a(k):
        p = order[k]
        s = p % cols
        if k == 0:
            for off in range(1, cols):
                code_a(off, (c - off + cols) % cols).wait_recv()
            for off in range(1, rows):
                code_b(off, (r - off + rows) % rows).wait_recv()
            inverse(codes_a, cap_a, keys_a, 0)
            inverse(codes_b, cap_b, keys_b, rows_a)
            move = pltpu.make_async_copy(inv_v, inv_s, local_sem)
            move.start()
            move.wait()
        if k % ratio == 0:
            own_a(s).wait()
            for off in range(1, cols):
                take_a(s, off).wait_recv()
        for lr in range(band_rows):
            for lk in range(band_rows):
                at = spot(lr * nb + p * band_rows + lk, 0)
                tiles_a[k % 2, lr * bs : (lr + 1) * bs, lk * bs : (lk + 1) * bs] = buf_a[s][at]

    def settle_b(k):
        p = order[k]
        own_b(p).wait()
        for chip in range(chips):
            take_across(p, chip).wait_recv()

    pair = 2 * bs

    def leave(n):
        where = pl.ds(n * pair, pair)
        return pltpu.make_async_copy(o_ref.at[:, where], out_ref.at[:, where], out_sem.at[n])

    def columns(k, n):
        p = order[k]
        for lk in range(band_rows):
            for half in range(2):
                at = spot((p * band_rows + lk) * band_cols + n * 2 + half, rows_a)
                tile_b[lk * bs : (lk + 1) * bs, half * bs : (half + 1) * bs] = buf_b[p][at]
        part = jnp.dot(tiles_a[k % 2], tile_b[...], preferred_element_type=jnp.float32)
        where = slice(n * pair, (n + 1) * pair)
        if k > 0:
            part = o_ref[:, where] + part
        if k < panels - 1:
            o_ref[:, where] = part
        else:
            for lr in range(band_rows):
                for half in range(2):
                    lc = n * 2 + half
                    o_ref[lr * bs : (lr + 1) * bs, lc * bs : (lc + 1) * bs] = part[
                        lr * bs : (lr + 1) * bs, half * bs : (half + 1) * bs
                    ] * mask_ref[lr, lc].astype(jnp.float32)
            leave(n).start()

    def work(k):
        parts = [functools.partial(settle_b, k)]
        if k < panels - 1:
            parts = [functools.partial(gather_a, k)] + parts
        return parts + [functools.partial(columns, k, n) for n in range(band_cols // 2)]

    for k, p in enumerate(order):
        s = p % cols
        if k + AHEAD < panels:
            start_own_b(order[k + AHEAD])
        if k % ratio == 0 and s + 2 < cols:
            start_a(s + 2)
        parts = work(k - 1) if k > 0 else []
        share = -(-len(parts) // (chips - 1))
        for d in range(1, chips):
            hop(p, d)
            for part in parts[(d - 1) * share : d * share]:
                part()
            if k == panels - 1 and d == max(chips - 2, 1):
                gather_a(k)
    for part in work(panels - 1):
        part()

    for n in range(band_cols // 2):
        leave(n).wait()
    for off in range(1, cols):
        code_a(off, c).wait_send()
        for s in range(cols):
            send_a(s, off).wait_send()
    for off in range(1, rows):
        code_b(off, r).wait_send()
    for p in order:
        for chip in range(chips):
            across(p, chip, False).wait_send()

            @pl.when((z < chips - 1) & (chip <= z))
            def _():
                along(p, chip, True, False).wait_send()

            @pl.when((z > 0) & (chip >= z))
            def _():
                along(p, chip, False, False).wait_send()


def shards(a_blocks, a_coord, b_blocks, b_coord, c_mask):
    rows = lax.axis_size("row")
    cols = lax.axis_size("col")
    slots, bs = a_blocks.shape[2], a_blocks.shape[-1]
    band_rows, band_cols = c_mask.shape
    chips = rows // 2
    nb = rows * band_rows
    a_tags = a_coord.reshape(slots, 2).T
    b_tags = b_coord.reshape(slots, 2).T
    inv_rows = (band_rows * nb + nb * band_cols) // 128
    inv_rows = (inv_rows + 7) // 8 * 8
    dma = pltpu.SemaphoreType.DMA
    wide, tall = band_cols * bs, band_rows * bs
    return pl.pallas_call(
        functools.partial(kernel, rows, cols, slots, band_rows, band_cols),
        out_shape=jax.ShapeDtypeStruct((tall, wide), jnp.float32),
        in_specs=[
            pl.BlockSpec(memory_space=pl.ANY),
            pl.BlockSpec(memory_space=pl.ANY),
            pl.BlockSpec(memory_space=pltpu.VMEM),
            pl.BlockSpec(memory_space=pltpu.VMEM),
            pl.BlockSpec(memory_space=pltpu.SMEM),
        ],
        out_specs=pl.BlockSpec(memory_space=pl.ANY),
        scratch_shapes=(
            [pltpu.VMEM((1 + slots, bs, bs), jnp.bfloat16)] * cols
            + [pltpu.VMEM((1 + slots, bs, bs), jnp.bfloat16)] * rows
            + [
                pltpu.VMEM((tall, wide), jnp.float32),
                dma((band_cols // 2,)),
                pltpu.VMEM((2, tall, tall), jnp.bfloat16),
                pltpu.VMEM((tall, 2 * bs), jnp.bfloat16),
                pltpu.VMEM((8, 128), jnp.int32),
                pltpu.VMEM((8, 128), jnp.int32),
                pltpu.VMEM((cols * 8, 128), jnp.int32),
                pltpu.VMEM((rows * 8, 128), jnp.int32),
                pltpu.VMEM((inv_rows, 128), jnp.int32),
                pltpu.SMEM((inv_rows, 128), jnp.int32),
                dma((cols,)), dma((rows,)),
                dma((cols, cols - 1)), dma((cols, cols - 1)),
                dma((cols - 1,)), dma((cols - 1,)),
                dma((rows - 1,)), dma((rows - 1,)),
                dma((rows, chips)), dma((rows, chips)), dma((rows, chips)),
                dma((rows, chips)), dma((rows, chips)),
                dma,
            ]
        ),
        compiler_params=pltpu.CompilerParams(
            collective_id=0, has_side_effects=True, vmem_limit_bytes=62 * 2**20),
        cost_estimate=pl.CostEstimate(
            flops=2 * tall * wide * nb * bs, transcendentals=0,
            bytes_accessed=(cols + rows) * slots * bs * bs * 2 + tall * wide * 4),
    )(a_blocks.reshape(slots, bs, bs), b_blocks.reshape(slots, bs, bs), a_tags, b_tags, c_mask)


def solution(mesh):
    placed = (
        P("row", "col", None, None, None),
        P("row", "col", None, None),
        P("row", "col", None, None, None),
        P("row", "col", None, None),
        P("row", "col"),
    )
    return jax.shard_map(
        shards, mesh=mesh, in_specs=placed, out_specs=P("row", "col"), check_vma=False
    )
```
